512 devices in a mesh: dp: 32 (over z, core), tp: 16 (over y, x).
Axes of the slice: x: 4, y: 4, z: 16, core: 2. Of those that a mesh axis runs over, the one named last changes fastest.
Arguments:
- residual_rows: bfloat16 [4096, 7168], P(('dp', 'tp')), may hold values from -6 to 6
- norm_gain: float32 [7168], replicated, may hold values from 0.25 to 1.75
- gate_weight: bfloat16 [7168, 10240], P(None, 'tp'), may hold values from -0.0625 to 0.0625
- up_weight: bfloat16 [7168, 10240], P(None, 'tp'), may hold values from -0.0625 to 0.0625
- down_weight: bfloat16 [10240, 7168], P('tp', 'dp'), may hold values from -0.0625 to 0.0625
- row_count: int32 [512], P(('dp', 'tp')), may hold values from 1 to 8, as said below
Outputs:
- layer_out: bfloat16 [4096, 7168], P(('dp', 'tp'))
The draws below stay inside these ranges and needn't reach their ends.
Inputs may be any that keep to these rules, and one draw needn't show every extreme that they name: `row_count`: every rank has at least one live row; some rank fills all 8 slots.
All inputs are finite; a program needn't handle non-finite values.
Results may differ from the reference program's by a relative error of at most 0.0046.
Values may be sent and summed in bfloat16 or wider, within the bound.
No kernel may reach another device: no remote copies, remote signals or barrier semaphores. Data moves between devices by JAX's collectives and lax.ppermute only.
A program may use at most 128 MiB of HBM per device.

```python
import jax
import jax.numpy as jnp
from jax import lax

D = 7168
FF = 10240
CAP = 8
RANKS = 512
TOKENS = 4096


def draw_row_count(key, part):
    key = jax.random.fold_in(key, 11)
    first, second = jax.random.split(key)
    counts = jax.random.randint(first, (RANKS,), 1, CAP + 1)
    chosen = jax.random.randint(second, (), 0, RANKS)
    return jnp.where(jnp.arange(RANKS) == chosen, CAP, counts).astype(jnp.int32)


def shard_levels(rng, dims, shards, least, largest):
    factor_of, own = 1.0, jax.random.fold_in(rng, 6)
    for dim, blocks in shards:
        draws = jnp.exp(jax.random.uniform(jax.random.fold_in(own, dim), (blocks,), jnp.float32, least / len(shards), largest / len(shards)))
        factor_of = factor_of * jnp.repeat(draws, dims[dim] // blocks).reshape([-1 if axis == dim else 1 for axis in range(len(dims))])
    return factor_of


def centred(own_key, shape, width, limit, pieces=(), held_as=jnp.bfloat16):
    values = jax.random.normal(own_key, shape, jnp.float32) * width
    if len(pieces) > 0:
        values = shard_levels(own_key, shape, pieces, -0.22, 0.18) * values
    return jnp.clip(values, min=-limit, max=limit).astype(held_as)


def setup_inputs(seed: int = 0) -> dict:
    streams_of = jax.random.split(jax.random.key(seed), 7)
    return {
        "residual_rows": centred(streams_of[0], (TOKENS, D), 1.0, 6.0, ((0, 512),)),
        "norm_gain": jnp.clip(1.0 + 0.15 * jax.random.normal(streams_of[1], (D,), jnp.float32), 0.25, 1.75),
        "gate_weight": centred(streams_of[2], (D, FF), D ** -0.5, 0.0625, ((1, 16),)),
        "up_weight": centred(streams_of[3], (D, FF), D ** -0.5, 0.0625, ((1, 16),)),
        "down_weight": centred(streams_of[4], (FF, D), FF ** -0.5, 0.0625, ((0, 16), (1, 32))),
        "row_count": draw_row_count(jax.random.fold_in(streams_of[6], 71), 0),
    }


def reference(residual_rows, norm_gain, gate_weight, up_weight, down_weight, row_count):
    resid = residual_rows.astype(jnp.float32)
    scale = jax.lax.rsqrt(lax.optimization_barrier(jnp.mean(resid * resid, axis=1, keepdims=True)) + 1e-06)
    normed = (resid * scale * norm_gain[None, :]).astype(jnp.bfloat16)
    gate = jnp.dot(normed, gate_weight, preferred_element_type=jnp.float32)
    up = jnp.dot(normed, up_weight, preferred_element_type=jnp.float32)
    hidden = (jax.nn.silu(gate) * up).astype(jnp.bfloat16)
    ffn = jnp.dot(hidden, down_weight, preferred_element_type=jnp.float32)
    slots = jnp.arange(TOKENS, dtype=jnp.int32) % CAP
    owner = jnp.arange(TOKENS, dtype=jnp.int32) // CAP
    live = (slots < row_count[owner]).astype(jnp.float32)[:, None]
    return (live * (resid + ffn)).astype(jnp.bfloat16)
```

```python
import jax
import jax.numpy as jnp
from jax import lax
from jax.sharding import PartitionSpec as P


def normalize(resid, norm_gain):
    scale = lax.rsqrt(jnp.mean(resid * resid, axis=1, keepdims=True) + 1e-06)
    return (resid * scale * norm_gain[None, :]).astype(jnp.bfloat16)


def shards(residual_rows, norm_gain, gate_weight, up_weight, down_weight, row_count):
    own_rows, width = residual_rows.shape
    ranks = lax.axis_size("tp")
    resid = residual_rows.astype(jnp.float32)
    down = lax.all_gather(down_weight, "dp", axis=1, tiled=True)
    normed = jnp.broadcast_to(normalize(resid, norm_gain)[None], (ranks, own_rows, width))
    gathered = lax.all_to_all(normed, "tp", 0, 0).reshape(ranks * own_rows, width)
    gate = jnp.dot(gathered, gate_weight, preferred_element_type=jnp.float32)
    up = jnp.dot(gathered, up_weight, preferred_element_type=jnp.float32)
    hidden = (jax.nn.silu(gate) * up).astype(jnp.bfloat16)
    partial_terms = jnp.dot(hidden, down, preferred_element_type=jnp.float32)
    partial_terms = partial_terms.astype(jnp.bfloat16).reshape(ranks, own_rows, width)
    terms = lax.all_to_all(partial_terms, "tp", 0, 0)
    ffn = jnp.sum(terms.astype(jnp.float32), axis=0)
    slots = jnp.arange(own_rows, dtype=jnp.int32)
    live = (slots < row_count[0]).astype(jnp.float32)[:, None]
    return (live * (resid + ffn)).astype(jnp.bfloat16)


def solution(mesh):
    return jax.shard_map(
        shards,
        mesh=mesh,
        in_specs=(
            P(("dp", "tp"), None),
            P(),
            P(None, "tp"),
            P(None, "tp"),
            P("tp", "dp"),
            P(("dp", "tp")),
        ),
        out_specs=P(("dp", "tp"), None),
        check_vma=False,
    )
```

```python
import jax
import jax.numpy as jnp
from jax import lax
from jax.sharding import PartitionSpec as P


def normalize(resid, norm_gain):
    scale = lax.rsqrt(jnp.mean(resid * resid, axis=1, keepdims=True) + 1e-06)
    return (resid * scale * norm_gain[None, :]).astype(jnp.bfloat16)


def shards(residual_rows, norm_gain, gate_weight, up_weight, down_weight, row_count):
    own_rows, width = residual_rows.shape
    ranks = lax.axis_size("tp")
    resid = residual_rows.astype(jnp.float32)
    down = lax.all_gather(down_weight, "dp", axis=1, tiled=True)
    normed = jnp.broadcast_to(normalize(resid, norm_gain)[None], (ranks, own_rows, width))
    gathered = lax.all_to_all(normed, "tp", 0, 0).reshape(ranks * own_rows, width)
    gate = jnp.dot(gathered, gate_weight, preferred_element_type=jnp.float32)
    up = jnp.dot(gathered, up_weight, preferred_element_type=jnp.float32)
    hidden = lax.optimization_barrier((jax.nn.silu(gate) * up).astype(jnp.bfloat16))
    partial_terms = jnp.dot(hidden, down, preferred_element_type=jnp.float32)
    partial_terms = partial_terms.astype(jnp.bfloat16).reshape(ranks, own_rows, width)
    slots = jnp.arange(own_rows, dtype=jnp.int32)
    live = (slots < row_count[0]).astype(jnp.float32)[:, None]
    partial_terms, resid, live = lax.optimization_barrier((partial_terms, resid, live))
    terms = lax.all_to_all(partial_terms, "tp", 0, 0)
    ffn = jnp.sum(terms.astype(jnp.float32), axis=0)
    return (live * (resid + ffn)).astype(jnp.bfloat16)


def solution(mesh):
    return jax.shard_map(
        shards,
        mesh=mesh,
        in_specs=(
            P(("dp", "tp"), None),
            P(),
            P(None, "tp"),
            P(None, "tp"),
            P("tp", "dp"),
            P(("dp", "tp")),
        ),
        out_specs=P(("dp", "tp"), None),
        check_vma=False,
    )
```

```python
import functools

import jax
import jax.numpy as jnp
from jax import lax
from jax.experimental import pallas as pl
from jax.experimental.pallas import tpu as pltpu
from jax.sharding import PartitionSpec as P

CORES = 2
NEAR = (-2, -1, 0, 1, 2)


def normalize(resid, norm_gain):
    scale = lax.rsqrt(jnp.mean(resid * resid, axis=1, keepdims=True) + 1e-06)
    return (resid * scale * norm_gain[None, :]).astype(jnp.bfloat16)


def dot_t(a, b):
    return lax.dot_general(a, b, (((1,), (1,)), ((), ())), preferred_element_type=jnp.float32)


def far_kernel(chips, first, count, hidden_ref, down_ref, out_ref, held, sems):
    features = held.shape[0] // count
    z = lax.axis_index("dp") // CORES
    copies = []
    for i in range(count):
        start = pl.multiple_of(lax.rem(z + (first + i), chips) * features, features)
        copy = pltpu.make_async_copy(
            down_ref.at[pl.ds(start, features), :],
            held.at[pl.ds(i * features, features), :],
            sems.at[i],
        )
        copy.start()
        copies.append(copy)
    for i in range(0, count, 2):
        stop = min(i + 2, count)
        for copy in copies[i:stop]:
            copy.wait()
        part = slice(i * features, stop * features)
        out_ref[:, part] = dot_t(hidden_ref[...], held[part, :]).astype(out_ref.dtype)


def far_terms(hidden, down, chips, first, count):
    rows, units = hidden.shape
    features = down.shape[0] // chips
    width = count * features
    return pl.pallas_call(
        functools.partial(far_kernel, chips, first, count),
        out_shape=jax.ShapeDtypeStruct((rows, width), jnp.bfloat16),
        in_specs=[pl.BlockSpec(memory_space=pltpu.VMEM), pl.BlockSpec(memory_space=pl.ANY)],
        out_specs=pl.BlockSpec(memory_space=pltpu.VMEM),
        scratch_shapes=[pltpu.VMEM((width, units), jnp.bfloat16), pltpu.SemaphoreType.DMA((count,))],
        compiler_params=pltpu.CompilerParams(vmem_limit_bytes=24 * 1024 * 1024),
        cost_estimate=pl.CostEstimate(
            flops=2 * rows * units * width, bytes_accessed=2 * width * (units + rows), transcendentals=0
        ),
        name="far_terms",
    )(hidden, down)


def summed(terms, ranks, own_rows):
    received = lax.all_to_all(terms.reshape(ranks, own_rows, -1), "tp", 0, 0)
    return jnp.sum(received.astype(jnp.float32), axis=0)


def shards(residual_rows, norm_gain, gate_weight, up_weight, down_weight, row_count):
    own_rows, width = residual_rows.shape
    ranks, groups = lax.axis_size("tp"), lax.axis_size("dp")
    chips = groups // CORES
    dp = lax.axis_index("dp")
    z, core = dp // CORES, dp % CORES
    resid = residual_rows.astype(jnp.float32)

    own = down_weight.T
    down = lax.all_gather(own, "dp", axis=0, tiled=True)

    def from_chip(step):
        if step == 0:
            return own
        return lax.ppermute(
            own, "dp", [((i + step * CORES) % groups, i) for i in range(groups)]
        )

    near = jnp.concatenate([from_chip(step) for step in NEAR], axis=0)
    near_other = lax.ppermute(near, "dp", [(i ^ 1, i) for i in range(groups)])

    normed = jnp.broadcast_to(normalize(resid, norm_gain)[None], (ranks, own_rows, width))
    gathered = lax.all_to_all(normed, "tp", 0, 0).reshape(ranks * own_rows, width)
    gate = jnp.dot(gathered, gate_weight, preferred_element_type=jnp.float32)
    up = jnp.dot(gathered, up_weight, preferred_element_type=jnp.float32)
    hidden = lax.optimization_barrier((jax.nn.silu(gate) * up).astype(jnp.bfloat16))

    near_terms = jnp.concatenate([dot_t(hidden, near), dot_t(hidden, near_other)], axis=1)
    near_sum = summed(near_terms.astype(jnp.bfloat16), ranks, own_rows)
    mine, other = jnp.split(near_sum.reshape(own_rows, CORES * len(NEAR), -1), 2, axis=1)
    first, second = jnp.where(core == 0, mine, other), jnp.where(core == 0, other, mine)
    near_sum = jnp.stack([first, second], axis=2).reshape(own_rows, -1)
    near_sum, hidden = lax.optimization_barrier((near_sum, hidden))

    far = far_terms(hidden, down, chips, NEAR[-1] + 1, chips - len(NEAR))
    slots = jnp.arange(own_rows, dtype=jnp.int32)
    live = (slots < row_count[0]).astype(jnp.float32)[:, None]
    far, resid, live = lax.optimization_barrier((far, resid, live))
    far_sum = summed(far, ranks, own_rows)
    ffn = jnp.roll(jnp.concatenate([near_sum, far_sum], axis=1), (z + NEAR[0]) * (width // chips), axis=1)
    return (live * (resid + ffn)).astype(jnp.bfloat16)


def solution(mesh):
    return jax.shard_map(
        shards,
        mesh=mesh,
        in_specs=(
            P(("dp", "tp"), None),
            P(),
            P(None, "tp"),
            P(None, "tp"),
            P("tp", "dp"),
            P(("dp", "tp")),
        ),
        out_specs=P(("dp", "tp"), None),
        check_vma=False,
    )
```

```python
import functools

import jax
import jax.numpy as jnp
from jax import lax
from jax.experimental import pallas as pl
from jax.experimental.pallas import tpu as pltpu
from jax.sharding import PartitionSpec as P

LANES = 128
PADDED = 16
STEP = 2


def normalize(resid, norm_gain):
    scale = lax.rsqrt(jnp.mean(resid * resid, axis=1, keepdims=True) + 1e-06)
    return (resid * scale * norm_gain[None, :]).astype(jnp.bfloat16)


def down_kernel(hidden_ref, down_ref, out_ref):
    @pl.when(pl.program_id(0) == 0)
    def _():
        out_ref[...] = jnp.zeros_like(out_ref)

    total = out_ref[...]
    for i in range(STEP):
        block = down_ref[:, i].reshape(out_ref.shape[1], down_ref.shape[3])
        total += lax.dot_general(
            hidden_ref[i], block, (((1,), (1,)), ((), ())), preferred_element_type=jnp.float32
        )
    out_ref[...] = total


def down_projection(hidden, down):
    ranks, rows, units = hidden.shape
    groups = down.shape[0]
    features = groups * PADDED
    return pl.pallas_call(
        down_kernel,
        grid=(ranks // STEP,),
        out_shape=jax.ShapeDtypeStruct((rows, features), jnp.float32),
        in_specs=[
            pl.BlockSpec((STEP, rows, units), lambda i: (i, 0, 0)),
            pl.BlockSpec((groups, STEP, PADDED, units), lambda i: (0, i, 0, 0)),
        ],
        out_specs=pl.BlockSpec((rows, features), lambda i: (0, 0)),
        compiler_params=pltpu.CompilerParams(vmem_limit_bytes=56 * 1024 * 1024),
        cost_estimate=pl.CostEstimate(
            flops=2 * rows * ranks * units * features,
            bytes_accessed=2 * ranks * units * (features + rows),
            transcendentals=0,
        ),
        name="down_projection",
    )(hidden, down)


def order_kernel(groups, each, parts_ref, out_ref):
    ranks, rows = parts_ref.shape[:2]
    lane = lax.broadcasted_iota(jnp.int32, (rows, LANES), 1)
    tiles = {}

    def put(tile, start, stop, value):
        if tile not in tiles:
            tiles[tile] = value
        else:
            tiles[tile] = jnp.where((lane >= start) & (lane < stop), value, tiles[tile])

    done = 0
    for group in range(groups):
        source = group * PADDED
        for rank in range(ranks):
            target = (group * ranks + rank) * each
            tile, start = divmod(target, LANES)
            first = source // LANES * LANES
            value = parts_ref[rank, :, first : first + LANES]
            value = pltpu.roll(value, (start - source % LANES) % LANES, 1)
            put(tile, start, min(start + each, LANES), value)
            if start + each > LANES:
                put(tile + 1, 0, start + each - LANES, value)
            while done < tile or (done in tiles and (done + 1) * LANES <= target + each):
                out_ref[:, done * LANES : (done + 1) * LANES] = tiles.pop(done)
                done += 1


def in_order(parts, groups, each):
    ranks, rows, _ = parts.shape
    return pl.pallas_call(
        functools.partial(order_kernel, groups, each),
        out_shape=jax.ShapeDtypeStruct((rows, groups * ranks * each), jnp.float32),
        in_specs=[pl.BlockSpec(memory_space=pltpu.VMEM)],
        out_specs=pl.BlockSpec(memory_space=pltpu.VMEM),
        name="in_order",
    )(parts)


def to_all(x, ranks):
    return lax.all_to_all(jnp.broadcast_to(x[None], (ranks, *x.shape)), "tp", 0, 0)


def shards(residual_rows, norm_gain, gate_weight, up_weight, down_weight, row_count):
    own_rows, width = residual_rows.shape
    ranks, groups = lax.axis_size("tp"), lax.axis_size("dp")
    units, features = down_weight.shape
    each = features // ranks
    resid = residual_rows.astype(jnp.float32)

    split = jnp.pad(down_weight.T.reshape(ranks, each, units), ((0, 0), (0, PADDED - each), (0, 0)))
    mine = lax.all_to_all(split, "tp", 0, 0)
    down = lax.all_gather(mine, "dp", axis=0, tiled=False)

    normed, mine = lax.optimization_barrier((normalize(resid, norm_gain), mine))
    gathered = to_all(normed, ranks).reshape(ranks * own_rows, width)
    gate = jnp.dot(gathered, gate_weight, preferred_element_type=jnp.float32)
    up = jnp.dot(gathered, up_weight, preferred_element_type=jnp.float32)
    hidden = (jax.nn.silu(gate) * up).astype(jnp.bfloat16)
    hidden, resid = lax.optimization_barrier((to_all(hidden, ranks), resid))

    total = down_projection(hidden, down)
    total, resid = lax.optimization_barrier((total, resid))
    parts = lax.all_to_all(total.reshape(ranks, own_rows, -1), "tp", 0, 0)
    ffn = in_order(parts, groups, each)
    slots = jnp.arange(own_rows, dtype=jnp.int32)
    live = (slots < row_count[0]).astype(jnp.float32)[:, None]
    return (live * (resid + ffn)).astype(jnp.bfloat16)


def solution(mesh):
    return jax.shard_map(
        shards,
        mesh=mesh,
        in_specs=(
            P(("dp", "tp"), None),
            P(),
            P(None, "tp"),
            P(None, "tp"),
            P("tp", "dp"),
            P(("dp", "tp")),
        ),
        out_specs=P(("dp", "tp"), None),
        check_vma=False,
    )
```

```python
import functools

import jax
import jax.numpy as jnp
from jax import lax
from jax.experimental import pallas as pl
from jax.experimental.pallas import tpu as pltpu
from jax.sharding import PartitionSpec as P

LANES = 128
PADDED = 16
STEP = 2


def normalize(resid, norm_gain):
    scale = lax.rsqrt(jnp.mean(resid * resid, axis=1, keepdims=True) + 1e-06)
    return (resid * scale * norm_gain[None, :]).astype(jnp.bfloat16)


def down_kernel(hidden_ref, down_ref, out_ref, total_ref):
    step = pl.program_id(0)
    features, rows = total_ref.shape
    units = down_ref.shape[3]
    block = jnp.concatenate([down_ref[:, i].reshape(features, units) for i in range(STEP)], axis=1)
    hidden = hidden_ref[...].reshape(STEP * units, rows)
    terms = jnp.dot(block, hidden, preferred_element_type=jnp.float32)

    @pl.when(step == 0)
    def _():
        total_ref[...] = terms

    @pl.when(step > 0)
    def _():
        total_ref[...] += terms

    @pl.when(step == pl.num_programs(0) - 1)
    def _():
        out_ref[...] = total_ref[...].T


def down_projection(hidden, down):
    ranks, units, rows = hidden.shape
    groups = down.shape[0]
    features = groups * PADDED
    return pl.pallas_call(
        down_kernel,
        grid=(ranks // STEP,),
        out_shape=jax.ShapeDtypeStruct((rows, features), jnp.float32),
        in_specs=[
            pl.BlockSpec((STEP, units, rows), lambda i: (i, 0, 0)),
            pl.BlockSpec((groups, STEP, PADDED, units), lambda i: (0, i, 0, 0)),
        ],
        out_specs=pl.BlockSpec((rows, features), lambda i: (0, 0)),
        scratch_shapes=[pltpu.VMEM((features, rows), jnp.float32)],
        compiler_params=pltpu.CompilerParams(vmem_limit_bytes=56 * 1024 * 1024),
        cost_estimate=pl.CostEstimate(
            flops=2 * rows * ranks * units * features,
            bytes_accessed=2 * ranks * units * (features + rows),
            transcendentals=0,
        ),
        name="down_projection",
    )(hidden, down)


def finish_kernel(groups, each, count_ref, parts_ref, resid_ref, out_ref):
    ranks, rows = parts_ref.shape[:2]
    slots = lax.broadcasted_iota(jnp.int32, (rows, LANES), 0)
    live = (slots < count_ref[0]).astype(jnp.float32)
    lane = lax.broadcasted_iota(jnp.int32, (rows, LANES), 1)
    tiles = {}

    def put(tile, start, stop, value):
        if tile not in tiles:
            tiles[tile] = value
        else:
            tiles[tile] = jnp.where((lane >= start) & (lane < stop), value, tiles[tile])

    done = 0
    for group in range(groups):
        source = group * PADDED
        for rank in range(ranks):
            target = (group * ranks + rank) * each
            tile, start = divmod(target, LANES)
            first = source // LANES * LANES
            value = parts_ref[rank, :, first : first + LANES]
            value = pltpu.roll(value, (start - source % LANES) % LANES, 1)
            put(tile, start, min(start + each, LANES), value)
            if start + each > LANES:
                put(tile + 1, 0, start + each - LANES, value)
            while done < tile or (done in tiles and (done + 1) * LANES <= target + each):
                part = slice(done * LANES, (done + 1) * LANES)
                resid = resid_ref[:, part].astype(jnp.float32)
                out_ref[:, part] = (live * (resid + tiles.pop(done))).astype(out_ref.dtype)
                done += 1


def finish(row_count, parts, residual_rows, groups, each):
    return pl.pallas_call(
        functools.partial(finish_kernel, groups, each),
        out_shape=jax.ShapeDtypeStruct(residual_rows.shape, residual_rows.dtype),
        in_specs=[
            pl.BlockSpec(memory_space=pltpu.SMEM),
            pl.BlockSpec(memory_space=pltpu.VMEM),
            pl.BlockSpec(memory_space=pltpu.VMEM),
        ],
        out_specs=pl.BlockSpec(memory_space=pltpu.VMEM),
        name="finish",
    )(row_count, parts, residual_rows)


def to_all(x, ranks):
    return lax.all_to_all(jnp.broadcast_to(x[None], (ranks, *x.shape)), "tp", 0, 0)


def shards(residual_rows, norm_gain, gate_weight, up_weight, down_weight, row_count):
    own_rows, width = residual_rows.shape
    ranks, groups = lax.axis_size("tp"), lax.axis_size("dp")
    units, features = down_weight.shape
    each = features // ranks
    resid = residual_rows.astype(jnp.float32)

    split = jnp.pad(down_weight.T.reshape(ranks, each, units), ((0, 0), (0, PADDED - each), (0, 0)))
    mine = lax.all_to_all(split, "tp", 0, 0)
    down = lax.all_gather(mine, "dp", axis=0, tiled=False)

    normed, mine = lax.optimization_barrier((normalize(resid, norm_gain), mine))
    gathered = to_all(normed, ranks).reshape(ranks * own_rows, width)
    gate = jnp.dot(gathered, gate_weight, preferred_element_type=jnp.float32)
    up = jnp.dot(gathered, up_weight, preferred_element_type=jnp.float32)
    hidden = (jax.nn.silu(gate) * up).astype(jnp.bfloat16)
    hidden = to_all(hidden.T, ranks)

    total = down_projection(hidden, down)
    total, residual_rows, row_count = lax.optimization_barrier((total, residual_rows, row_count))
    parts = lax.all_to_all(total.reshape(ranks, own_rows, -1), "tp", 0, 0)
    return finish(row_count, parts, residual_rows, groups, each)


def solution(mesh):
    return jax.shard_map(
        shards,
        mesh=mesh,
        in_specs=(
            P(("dp", "tp"), None),
            P(),
            P(None, "tp"),
            P(None, "tp"),
            P("tp", "dp"),
            P(("dp", "tp")),
        ),
        out_specs=P(("dp", "tp"), None),
        check_vma=False,
    )
```

```python
import functools

import jax
import jax.numpy as jnp
from jax import lax
from jax.experimental import pallas as pl
from jax.experimental.pallas import tpu as pltpu
from jax.sharding import PartitionSpec as P

LANES = 128
PADDED = 16
CHUNK = 8
VMEM_LIMIT = 56 * 1024 * 1024


def normalize(resid, norm_gain):
    scale = lax.rsqrt(jnp.mean(resid * resid, axis=1, keepdims=True) + 1e-06)
    return (resid * scale * norm_gain[None, :]).astype(jnp.bfloat16)


def down_kernel(hidden_ref, down_ref, out_ref, held, sems):
    groups, ranks, padded, units = held.shape
    copies = []
    for i in range(groups // CHUNK):
        part = pl.ds(i * CHUNK, CHUNK)
        copy = pltpu.make_async_copy(down_ref.at[part], held.at[part], sems.at[i])
        copy.start()
        copies.append(copy)
    features = CHUNK * padded
    for i, copy in enumerate(copies):
        copy.wait()
        total = None
        for j in range(0, ranks, 2):
            block = jnp.concatenate(
                [held[i * CHUNK : (i + 1) * CHUNK, k].reshape(features, units) for k in (j, j + 1)], axis=1
            )
            hidden = hidden_ref[j : j + 2].reshape(2 * units, -1)
            terms = jnp.dot(block, hidden, preferred_element_type=jnp.float32)
            total = terms if total is None else total + terms
        out_ref[:, i * features : (i + 1) * features] = total.T


def down_projection(hidden, down):
    ranks, units, rows = hidden.shape
    groups = down.shape[0]
    features = groups * PADDED
    return pl.pallas_call(
        down_kernel,
        out_shape=jax.ShapeDtypeStruct((rows, features), jnp.float32),
        in_specs=[pl.BlockSpec(memory_space=pltpu.VMEM), pl.BlockSpec(memory_space=pl.ANY)],
        out_specs=pl.BlockSpec(memory_space=pltpu.VMEM),
        scratch_shapes=[
            pltpu.VMEM(down.shape, jnp.bfloat16),
            pltpu.SemaphoreType.DMA((groups // CHUNK,)),
        ],
        compiler_params=pltpu.CompilerParams(vmem_limit_bytes=VMEM_LIMIT),
        cost_estimate=pl.CostEstimate(
            flops=2 * rows * ranks * units * features,
            bytes_accessed=2 * ranks * units * (features + rows),
            transcendentals=0,
        ),
        name="down_projection",
    )(hidden, down)


def finish_kernel(groups, each, count_ref, parts_ref, resid_ref, out_ref, resid, ffn, sem):
    copy = pltpu.make_async_copy(resid_ref, resid, sem)
    copy.start()
    ranks, rows = parts_ref.shape[:2]
    slots = lax.broadcasted_iota(jnp.int32, (rows, LANES), 0)
    live = (slots < count_ref[0]).astype(jnp.float32)
    lane = lax.broadcasted_iota(jnp.int32, (rows, LANES), 1)
    tiles = {}

    def put(tile, start, stop, value):
        if tile not in tiles:
            tiles[tile] = value
        else:
            tiles[tile] = jnp.where((lane >= start) & (lane < stop), value, tiles[tile])

    done = 0
    for group in range(groups):
        source = group * PADDED
        for rank in range(ranks):
            target = (group * ranks + rank) * each
            tile, start = divmod(target, LANES)
            first = source // LANES * LANES
            value = parts_ref[rank, :, first : first + LANES]
            value = pltpu.roll(value, (start - source % LANES) % LANES, 1)
            put(tile, start, min(start + each, LANES), value)
            if start + each > LANES:
                put(tile + 1, 0, start + each - LANES, value)
            while done < tile or (done in tiles and (done + 1) * LANES <= target + each):
                ffn[:, done * LANES : (done + 1) * LANES] = tiles.pop(done)
                done += 1
    copy.wait()
    for i in range(done):
        part = slice(i * LANES, (i + 1) * LANES)
        out_ref[:, part] = (live * (resid[:, part] + ffn[:, part])).astype(out_ref.dtype)


def finish(row_count, parts, resid, groups, each):
    return pl.pallas_call(
        functools.partial(finish_kernel, groups, each),
        out_shape=jax.ShapeDtypeStruct(resid.shape, jnp.bfloat16),
        in_specs=[
            pl.BlockSpec(memory_space=pltpu.SMEM),
            pl.BlockSpec(memory_space=pltpu.VMEM),
            pl.BlockSpec(memory_space=pl.ANY),
        ],
        out_specs=pl.BlockSpec(memory_space=pltpu.VMEM),
        scratch_shapes=[
            pltpu.VMEM(resid.shape, jnp.float32),
            pltpu.VMEM(resid.shape, jnp.float32),
            pltpu.SemaphoreType.DMA,
        ],
        compiler_params=pltpu.CompilerParams(vmem_limit_bytes=VMEM_LIMIT),
        name="finish",
    )(row_count, parts, resid)


def to_all(x, ranks):
    return lax.all_to_all(jnp.broadcast_to(x[None], (ranks, *x.shape)), "tp", 0, 0)


def shards(residual_rows, norm_gain, gate_weight, up_weight, down_weight, row_count):
    own_rows, width = residual_rows.shape
    ranks, groups = lax.axis_size("tp"), lax.axis_size("dp")
    units, features = down_weight.shape
    each = features // ranks
    resid = residual_rows.astype(jnp.float32)

    split = jnp.pad(down_weight.T.reshape(ranks, each, units), ((0, 0), (0, PADDED - each), (0, 0)))
    mine = lax.all_to_all(split, "tp", 0, 0)
    down = lax.all_gather(mine, "dp", axis=0, tiled=False)

    normed, mine = lax.optimization_barrier((normalize(resid, norm_gain), mine))
    gathered = to_all(normed, ranks).reshape(ranks * own_rows, width)
    gate = jnp.dot(gathered, gate_weight, preferred_element_type=jnp.float32)
    up = jnp.dot(gathered, up_weight, preferred_element_type=jnp.float32)
    hidden = (jax.nn.silu(gate) * up).astype(jnp.bfloat16)
    hidden, resid = lax.optimization_barrier((hidden.T, resid))
    hidden = to_all(hidden, ranks)

    total = down_projection(hidden, down)
    total, resid, row_count = lax.optimization_barrier((total, resid, row_count))
    parts = lax.all_to_all(total.reshape(ranks, own_rows, -1), "tp", 0, 0)
    return finish(row_count, parts, resid, groups, each)


def solution(mesh):
    return jax.shard_map(
        shards,
        mesh=mesh,
        in_specs=(
            P(("dp", "tp"), None),
            P(),
            P(None, "tp"),
            P(None, "tp"),
            P("tp", "dp"),
            P(("dp", "tp")),
        ),
        out_specs=P(("dp", "tp"), None),
        check_vma=False,
    )
```

```python
import functools

import jax
import jax.numpy as jnp
from jax import lax
from jax.experimental import pallas as pl
from jax.experimental.pallas import tpu as pltpu
from jax.sharding import PartitionSpec as P

LANES = 128
PADDED = 16
CHUNK = 8
VMEM_LIMIT = 56 * 1024 * 1024


def normalize(resid, norm_gain):
    scale = lax.rsqrt(jnp.mean(resid * resid, axis=1, keepdims=True) + 1e-06)
    return (resid * scale * norm_gain[None, :]).astype(jnp.bfloat16)


def down_kernel(hidden_ref, down_ref, out_ref, held, sems):
    groups, ranks, padded, units = held.shape
    copies = []
    for i in range(groups // CHUNK):
        part = pl.ds(i * CHUNK, CHUNK)
        copy = pltpu.make_async_copy(down_ref.at[part], held.at[part], sems.at[i])
        copy.start()
        copies.append(copy)
    features = CHUNK * padded
    for i, copy in enumerate(copies):
        copy.wait()
        total = None
        for j in range(0, ranks, 2):
            block = jnp.concatenate(
                [held[i * CHUNK : (i + 1) * CHUNK, k].reshape(features, units) for k in (j, j + 1)], axis=1
            )
            hidden = hidden_ref[j : j + 2].reshape(2 * units, -1)
            terms = jnp.dot(block, hidden, preferred_element_type=jnp.float32)
            total = terms if total is None else total + terms
        out_ref[:, i * features : (i + 1) * features] = total.T


def down_projection(hidden, down):
    ranks, units, rows = hidden.shape
    groups = down.shape[0]
    features = groups * PADDED
    return pl.pallas_call(
        down_kernel,
        out_shape=jax.ShapeDtypeStruct((rows, features), jnp.float32),
        in_specs=[pl.BlockSpec(memory_space=pltpu.VMEM), pl.BlockSpec(memory_space=pl.ANY)],
        out_specs=pl.BlockSpec(memory_space=pltpu.VMEM),
        scratch_shapes=[
            pltpu.VMEM(down.shape, jnp.bfloat16),
            pltpu.SemaphoreType.DMA((groups // CHUNK,)),
        ],
        compiler_params=pltpu.CompilerParams(vmem_limit_bytes=VMEM_LIMIT),
        cost_estimate=pl.CostEstimate(
            flops=2 * rows * ranks * units * features,
            bytes_accessed=2 * ranks * units * (features + rows),
            transcendentals=0,
        ),
        name="down_projection",
    )(hidden, down)


def finish_kernel(groups, each, parts_ref, own_ref, out_ref, own, ffn, sem):
    copy = pltpu.make_async_copy(own_ref, own, sem)
    copy.start()
    ranks, rows = parts_ref.shape[:2]
    lane = lax.broadcasted_iota(jnp.int32, (rows, LANES), 1)
    tiles = {}

    def put(tile, start, stop, value):
        if tile not in tiles:
            tiles[tile] = value
        else:
            tiles[tile] = jnp.where((lane >= start) & (lane < stop), value, tiles[tile])

    done = 0
    for group in range(groups):
        source = group * PADDED
        for rank in range(ranks):
            target = (group * ranks + rank) * each
            tile, start = divmod(target, LANES)
            first = source // LANES * LANES
            value = parts_ref[rank, :, first : first + LANES]
            value = pltpu.roll(value, (start - source % LANES) % LANES, 1)
            put(tile, start, min(start + each, LANES), value)
            if start + each > LANES:
                put(tile + 1, 0, start + each - LANES, value)
            while done < tile or (done in tiles and (done + 1) * LANES <= target + each):
                ffn[:, done * LANES : (done + 1) * LANES] = tiles.pop(done)
                done += 1
    copy.wait()
    live = own[:, done * LANES :]
    for i in range(done):
        part = slice(i * LANES, (i + 1) * LANES)
        out_ref[:, part] = (live * (own[:, part] + ffn[:, part])).astype(out_ref.dtype)


def finish(parts, own, groups, each):
    rows, width = own.shape[0], own.shape[1] - LANES
    return pl.pallas_call(
        functools.partial(finish_kernel, groups, each),
        out_shape=jax.ShapeDtypeStruct((rows, width), jnp.bfloat16),
        in_specs=[pl.BlockSpec(memory_space=pltpu.VMEM), pl.BlockSpec(memory_space=pl.ANY)],
        out_specs=pl.BlockSpec(memory_space=pltpu.VMEM),
        scratch_shapes=[
            pltpu.VMEM(own.shape, jnp.float32),
            pltpu.VMEM((rows, width), jnp.float32),
            pltpu.SemaphoreType.DMA,
        ],
        name="finish",
    )(parts, own)


def to_all(x, ranks):
    return lax.all_to_all(jnp.broadcast_to(x[None], (ranks, *x.shape)), "tp", 0, 0)


def shards(residual_rows, norm_gain, gate_weight, up_weight, down_weight, row_count):
    own_rows, width = residual_rows.shape
    ranks, groups = lax.axis_size("tp"), lax.axis_size("dp")
    units, features = down_weight.shape
    each = features // ranks
    resid = residual_rows.astype(jnp.float32)

    split = jnp.pad(down_weight.T.reshape(ranks, each, units), ((0, 0), (0, PADDED - each), (0, 0)))
    mine = lax.all_to_all(split, "tp", 0, 0)
    down = lax.all_gather(mine, "dp", axis=0, tiled=False)

    normed, mine = lax.optimization_barrier((normalize(resid, norm_gain), mine))
    gathered = to_all(normed, ranks).reshape(ranks * own_rows, width)
    gathered, residual_rows, row_count = lax.optimization_barrier((gathered, residual_rows, row_count))
    gate = jnp.dot(gathered, gate_weight, preferred_element_type=jnp.float32)
    up = jnp.dot(gathered, up_weight, preferred_element_type=jnp.float32)
    hidden = (jax.nn.silu(gate) * up).astype(jnp.bfloat16)
    live = lax.broadcasted_iota(jnp.int32, (own_rows, LANES), 0) < row_count[0]
    own = jnp.concatenate([residual_rows.astype(jnp.float32), live.astype(jnp.float32)], axis=1)
    hidden, own = lax.optimization_barrier((hidden.T, own))
    hidden = to_all(hidden, ranks)

    total = down_projection(hidden, down)
    parts = lax.all_to_all(total.reshape(ranks, own_rows, -1), "tp", 0, 0)
    return finish(parts, own, groups, each)


def solution(mesh):
    return jax.shard_map(
        shards,
        mesh=mesh,
        in_specs=(
            P(("dp", "tp"), None),
            P(),
            P(None, "tp"),
            P(None, "tp"),
            P("tp", "dp"),
            P(("dp", "tp")),
        ),
        out_specs=P(("dp", "tp"), None),
        check_vma=False,
    )
```

```python
import functools

import jax
import jax.numpy as jnp
from jax import lax
from jax.experimental import pallas as pl
from jax.experimental.pallas import tpu as pltpu
from jax.sharding import PartitionSpec as P

LANES = 128
PADDED = 16
CORES = 2
CHUNK = 8


def normalize(resid, norm_gain):
    scale = lax.rsqrt(jnp.mean(resid * resid, axis=1, keepdims=True) + 1e-06)
    return (resid * scale * norm_gain[None, :]).astype(jnp.bfloat16)


def down_kernel(hidden_ref, other_ref, down_ref, out_ref, other_out_ref, held, sems):
    chips, ranks, padded, units = held.shape
    rows = hidden_ref.shape[2]
    copies = []
    for i in range(chips // CHUNK):
        part = pl.ds(i * CHUNK, CHUNK)
        copy = pltpu.make_async_copy(down_ref.at[part], held.at[part], sems.at[i])
        copy.start()
        copies.append(copy)
    features = CHUNK * padded
    for i, copy in enumerate(copies):
        copy.wait()
        total = None
        for j in range(0, ranks, 2):
            block = jnp.concatenate(
                [held[i * CHUNK : (i + 1) * CHUNK, k].reshape(features, units) for k in (j, j + 1)], axis=1
            )
            hidden = jnp.concatenate(
                [ref[j : j + 2].reshape(2 * units, rows) for ref in (hidden_ref, other_ref)], axis=1
            )
            terms = jnp.dot(block, hidden, preferred_element_type=jnp.float32)
            total = terms if total is None else total + terms
        part = slice(i * features, (i + 1) * features)
        out_ref[:, part] = total[:, :rows].T
        other_out_ref[:, part] = total[:, rows:].T


def down_projection(hidden, other, down):
    ranks, units, rows = hidden.shape
    chips = down.shape[0]
    features = chips * PADDED
    in_vmem = pl.BlockSpec(memory_space=pltpu.VMEM)
    return pl.pallas_call(
        down_kernel,
        out_shape=[jax.ShapeDtypeStruct((rows, features), jnp.float32)] * 2,
        in_specs=[in_vmem, in_vmem, pl.BlockSpec(memory_space=pl.ANY)],
        out_specs=[in_vmem, in_vmem],
        scratch_shapes=[
            pltpu.VMEM(down.shape, jnp.bfloat16),
            pltpu.SemaphoreType.DMA((chips // CHUNK,)),
        ],
        compiler_params=pltpu.CompilerParams(vmem_limit_bytes=56 * 1024 * 1024),
        cost_estimate=pl.CostEstimate(
            flops=4 * rows * ranks * units * features,
            bytes_accessed=2 * ranks * units * (features + 2 * rows),
            transcendentals=0,
        ),
        name="down_projection",
    )(hidden, other, down)


def finish_kernel(groups, each, count_ref, parts_ref, resid_ref, out_ref):
    ranks, rows = parts_ref.shape[:2]
    slots = lax.broadcasted_iota(jnp.int32, (rows, LANES), 0)
    live = (slots < count_ref[0]).astype(jnp.float32)
    lane = lax.broadcasted_iota(jnp.int32, (rows, LANES), 1)
    first_core = lax.rem(lax.axis_index("dp"), CORES) == 0
    half = groups // CORES * PADDED
    held = {}
    for rank in range(ranks):
        for at in range(0, half, LANES):
            mine, other = (parts_ref[rank, :, i : i + LANES] for i in (at, half + at))
            held[rank, 0, at] = jnp.where(first_core, mine, other)
            held[rank, 1, at] = jnp.where(first_core, other, mine)
    tiles = {}

    def put(tile, start, stop, value):
        if tile not in tiles:
            tiles[tile] = value
        else:
            tiles[tile] = jnp.where((lane >= start) & (lane < stop), value, tiles[tile])

    done = 0
    for group in range(groups):
        source = group // CORES * PADDED
        for rank in range(ranks):
            target = (group * ranks + rank) * each
            tile, start = divmod(target, LANES)
            value = held[rank, group % CORES, source // LANES * LANES]
            value = pltpu.roll(value, (start - source % LANES) % LANES, 1)
            put(tile, start, min(start + each, LANES), value)
            if start + each > LANES:
                put(tile + 1, 0, start + each - LANES, value)
            while done < tile or (done in tiles and (done + 1) * LANES <= target + each):
                part = slice(done * LANES, (done + 1) * LANES)
                resid = resid_ref[:, part].astype(jnp.float32)
                out_ref[:, part] = (live * (resid + tiles.pop(done))).astype(out_ref.dtype)
                done += 1


def finish(row_count, parts, residual_rows, groups, each):
    return pl.pallas_call(
        functools.partial(finish_kernel, groups, each),
        out_shape=jax.ShapeDtypeStruct(residual_rows.shape, residual_rows.dtype),
        in_specs=[
            pl.BlockSpec(memory_space=pltpu.SMEM),
            pl.BlockSpec(memory_space=pltpu.VMEM),
            pl.BlockSpec(memory_space=pltpu.VMEM),
        ],
        out_specs=pl.BlockSpec(memory_space=pltpu.VMEM),
        name="finish",
    )(row_count, parts, residual_rows)


def to_all(x, ranks):
    return lax.all_to_all(jnp.broadcast_to(x[None], (ranks, *x.shape)), "tp", 0, 0)


def shards(residual_rows, norm_gain, gate_weight, up_weight, down_weight, row_count):
    own_rows, width = residual_rows.shape
    ranks, groups = lax.axis_size("tp"), lax.axis_size("dp")
    units, features = down_weight.shape
    each = features // ranks
    resid = residual_rows.astype(jnp.float32)

    split = jnp.pad(down_weight.T.reshape(ranks, each, units), ((0, 0), (0, PADDED - each), (0, 0)))
    mine = lax.all_to_all(split, "tp", 0, 0)
    same_core = [list(range(core, groups, CORES)) for core in range(CORES)]
    down = lax.all_gather(mine, "dp", axis=0, tiled=False, axis_index_groups=same_core)

    normed, mine = lax.optimization_barrier((normalize(resid, norm_gain), mine))
    gathered = to_all(normed, ranks).reshape(ranks * own_rows, width)
    gate = jnp.dot(gathered, gate_weight, preferred_element_type=jnp.float32)
    up = jnp.dot(gathered, up_weight, preferred_element_type=jnp.float32)
    hidden = (jax.nn.silu(gate) * up).astype(jnp.bfloat16)
    hidden = to_all(hidden.T, ranks)

    swap = [(i, i ^ 1) for i in range(groups)]
    total, others = down_projection(hidden, lax.ppermute(hidden, "dp", swap), down)
    total = jnp.concatenate([total, lax.ppermute(others, "dp", swap)], axis=1)
    total, residual_rows, row_count = lax.optimization_barrier((total, residual_rows, row_count))
    parts = lax.all_to_all(total.reshape(ranks, own_rows, -1), "tp", 0, 0)
    return finish(row_count, parts, residual_rows, groups, each)


def solution(mesh):
    return jax.shard_map(
        shards,
        mesh=mesh,
        in_specs=(
            P(("dp", "tp"), None),
            P(),
            P(None, "tp"),
            P(None, "tp"),
            P("tp", "dp"),
            P(("dp", "tp")),
        ),
        out_specs=P(("dp", "tp"), None),
        check_vma=False,
    )
```

```python
import functools

import jax
import jax.numpy as jnp
from jax import lax
from jax.experimental import pallas as pl
from jax.experimental.pallas import tpu as pltpu
from jax.sharding import PartitionSpec as P

LANES = 128
PADDED = 16
CHUNK = 8
VMEM_LIMIT = 52 * 1024 * 1024


def normalize(resid, norm_gain):
    scale = lax.rsqrt(jnp.mean(resid * resid, axis=1, keepdims=True) + 1e-06)
    return (resid * scale * norm_gain[None, :]).astype(jnp.bfloat16)


def down_kernel(hidden_ref, down_ref, out_ref, held, sems):
    groups, ranks, padded, units = held.shape
    copies = []
    for i in range(groups // CHUNK):
        part = pl.ds(i * CHUNK, CHUNK)
        copy = pltpu.make_async_copy(down_ref.at[part], held.at[part], sems.at[i])
        copy.start()
        copies.append(copy)
    features = CHUNK * padded
    for i, copy in enumerate(copies):
        copy.wait()
        total = None
        for j in range(0, ranks, 2):
            block = jnp.concatenate(
                [held[i * CHUNK : (i + 1) * CHUNK, k].reshape(features, units) for k in (j, j + 1)], axis=1
            )
            hidden = hidden_ref[j : j + 2].reshape(2 * units, -1)
            terms = jnp.dot(block, hidden, preferred_element_type=jnp.float32)
            total = terms if total is None else total + terms
        out_ref[:, i * features : (i + 1) * features] = total.T


def down_projection(hidden, down):
    ranks, units, rows = hidden.shape
    groups = down.shape[0]
    features = groups * PADDED
    return pl.pallas_call(
        down_kernel,
        out_shape=jax.ShapeDtypeStruct((rows, features), jnp.float32),
        in_specs=[pl.BlockSpec(memory_space=pltpu.VMEM), pl.BlockSpec(memory_space=pl.ANY)],
        out_specs=pl.BlockSpec(memory_space=pltpu.VMEM),
        scratch_shapes=[
            pltpu.VMEM(down.shape, jnp.bfloat16),
            pltpu.SemaphoreType.DMA((groups // CHUNK,)),
        ],
        compiler_params=pltpu.CompilerParams(vmem_limit_bytes=VMEM_LIMIT),
        cost_estimate=pl.CostEstimate(
            flops=2 * rows * ranks * units * features,
            bytes_accessed=2 * ranks * units * (features + rows),
            transcendentals=0,
        ),
        name="down_projection",
    )(hidden, down)


def finish_kernel(groups, each, parts_ref, own_ref, out_ref):
    ranks, rows = parts_ref.shape[:2]
    live = own_ref[:, out_ref.shape[1] :]
    lane = lax.broadcasted_iota(jnp.int32, (rows, LANES), 1)
    tiles = {}

    def put(tile, start, stop, value):
        if tile not in tiles:
            tiles[tile] = value
        else:
            tiles[tile] = jnp.where((lane >= start) & (lane < stop), value, tiles[tile])

    done = 0
    for group in range(groups):
        source = group * PADDED
        for rank in range(ranks):
            target = (group * ranks + rank) * each
            tile, start = divmod(target, LANES)
            first = source // LANES * LANES
            value = parts_ref[rank, :, first : first + LANES]
            value = pltpu.roll(value, (start - source % LANES) % LANES, 1)
            put(tile, start, min(start + each, LANES), value)
            if start + each > LANES:
                put(tile + 1, 0, start + each - LANES, value)
            while done < tile or (done in tiles and (done + 1) * LANES <= target + each):
                part = slice(done * LANES, (done + 1) * LANES)
                out_ref[:, part] = (live * (own_ref[:, part] + tiles.pop(done))).astype(out_ref.dtype)
                done += 1


def finish(parts, own, groups, each):
    rows, width = own.shape[0], own.shape[1] - LANES
    return pl.pallas_call(
        functools.partial(finish_kernel, groups, each),
        out_shape=jax.ShapeDtypeStruct((rows, width), jnp.bfloat16),
        in_specs=[pl.BlockSpec(memory_space=pltpu.VMEM)] * 2,
        out_specs=pl.BlockSpec(memory_space=pltpu.VMEM),
        name="finish",
    )(parts, own)


def to_all(x, ranks):
    return lax.all_to_all(jnp.broadcast_to(x[None], (ranks, *x.shape)), "tp", 0, 0)


def shards(residual_rows, norm_gain, gate_weight, up_weight, down_weight, row_count):
    own_rows, width = residual_rows.shape
    ranks, groups = lax.axis_size("tp"), lax.axis_size("dp")
    units, features = down_weight.shape
    each = features // ranks
    resid = residual_rows.astype(jnp.float32)

    split = jnp.pad(down_weight.T.reshape(ranks, each, units), ((0, 0), (0, PADDED - each), (0, 0)))
    mine = lax.all_to_all(split, "tp", 0, 0)
    down = lax.all_gather(mine, "dp", axis=0, tiled=False)

    normed, mine = lax.optimization_barrier((normalize(resid, norm_gain), mine))
    gathered = to_all(normed, ranks).reshape(ranks * own_rows, width)
    gathered, residual_rows, row_count = lax.optimization_barrier((gathered, residual_rows, row_count))
    gate = jnp.dot(gathered, gate_weight, preferred_element_type=jnp.float32)
    up = jnp.dot(gathered, up_weight, preferred_element_type=jnp.float32)
    hidden = (jax.nn.silu(gate) * up).astype(jnp.bfloat16)
    live = lax.broadcasted_iota(jnp.int32, (own_rows, LANES), 0) < row_count[0]
    own = jnp.concatenate([residual_rows.astype(jnp.float32), live.astype(jnp.float32)], axis=1)
    hidden, own = lax.optimization_barrier((hidden.T, own))
    hidden = to_all(hidden, ranks)

    total = down_projection(hidden, down)
    parts = lax.all_to_all(total.reshape(ranks, own_rows, -1), "tp", 0, 0)
    return finish(parts, own, groups, each)


def solution(mesh):
    return jax.shard_map(
        shards,
        mesh=mesh,
        in_specs=(
            P(("dp", "tp"), None),
            P(),
            P(None, "tp"),
            P(None, "tp"),
            P("tp", "dp"),
            P(("dp", "tp")),
        ),
        out_specs=P(("dp", "tp"), None),
        check_vma=False,
    )
```

```python
import functools

import jax
import jax.numpy as jnp
from jax import lax
from jax.experimental import pallas as pl
from jax.experimental.pallas import tpu as pltpu
from jax.sharding import PartitionSpec as P

LANES = 128
PADDED = 16
CHUNK = 8
VMEM_LIMIT = 46 * 1024 * 1024


def normalize(resid, norm_gain):
    scale = lax.rsqrt(jnp.mean(resid * resid, axis=1, keepdims=True) + 1e-06)
    return (resid * scale * norm_gain[None, :]).astype(jnp.bfloat16)


def fetch_kernel(x_ref, out_ref, sem):
    copy = pltpu.make_async_copy(x_ref, out_ref, sem)
    copy.start()
    copy.wait()


def fetched(x):
    return pl.pallas_call(
        fetch_kernel,
        out_shape=jax.ShapeDtypeStruct(x.shape, x.dtype),
        in_specs=[pl.BlockSpec(memory_space=pl.ANY)],
        out_specs=pl.BlockSpec(memory_space=pltpu.VMEM),
        scratch_shapes=[pltpu.SemaphoreType.DMA],
        cost_estimate=pl.CostEstimate(flops=0, bytes_accessed=2 * x.size * x.dtype.itemsize, transcendentals=0),
        name="fetched",
    )(x)


def down_kernel(groups, hidden_ref, down_ref, out_ref, held, sems):
    ranks, units = hidden_ref.shape[:2]
    size = CHUNK * ranks * PADDED
    copies = []
    for i in range(groups // CHUNK):
        part = pl.ds(i * size, size)
        copy = pltpu.make_async_copy(down_ref.at[part], held.at[part], sems.at[i])
        copy.start()
        copies.append(copy)
    features = CHUNK * PADDED
    for i, copy in enumerate(copies):
        copy.wait()

        def block(rank):
            starts = [i * size + (group * ranks + rank) * PADDED for group in range(CHUNK)]
            return jnp.concatenate([held[start : start + PADDED, :] for start in starts], axis=0)

        total = None
        for j in range(0, ranks, 2):
            both = jnp.concatenate([block(j), block(j + 1)], axis=1)
            hidden = hidden_ref[j : j + 2].reshape(2 * units, -1)
            terms = jnp.dot(both, hidden, preferred_element_type=jnp.float32)
            total = terms if total is None else total + terms
        out_ref[:, i * features : (i + 1) * features] = total.T


def down_projection(hidden, down):
    ranks, units, rows = hidden.shape
    groups = down.shape[0] // (ranks * PADDED)
    features = groups * PADDED
    return pl.pallas_call(
        functools.partial(down_kernel, groups),
        out_shape=jax.ShapeDtypeStruct((rows, features), jnp.float32),
        in_specs=[pl.BlockSpec(memory_space=pltpu.VMEM), pl.BlockSpec(memory_space=pl.ANY)],
        out_specs=pl.BlockSpec(memory_space=pltpu.VMEM),
        scratch_shapes=[
            pltpu.VMEM(down.shape, jnp.bfloat16),
            pltpu.SemaphoreType.DMA((groups // CHUNK,)),
        ],
        compiler_params=pltpu.CompilerParams(vmem_limit_bytes=VMEM_LIMIT),
        cost_estimate=pl.CostEstimate(
            flops=2 * rows * ranks * units * features,
            bytes_accessed=2 * ranks * units * (features + rows),
            transcendentals=0,
        ),
        name="down_projection",
    )(hidden, down)


def finish_kernel(groups, each, parts_ref, own_ref, out_ref):
    ranks, rows = parts_ref.shape[:2]
    live = own_ref[:, out_ref.shape[1] :]
    lane = lax.broadcasted_iota(jnp.int32, (rows, LANES), 1)
    tiles = {}

    def put(tile, start, stop, value):
        if tile not in tiles:
            tiles[tile] = value
        else:
            tiles[tile] = jnp.where((lane >= start) & (lane < stop), value, tiles[tile])

    done = 0
    for group in range(groups):
        source = group * PADDED
        for rank in range(ranks):
            target = (group * ranks + rank) * each
            tile, start = divmod(target, LANES)
            first = source // LANES * LANES
            value = parts_ref[rank, :, first : first + LANES]
            value = pltpu.roll(value, (start - source % LANES) % LANES, 1)
            put(tile, start, min(start + each, LANES), value)
            if start + each > LANES:
                put(tile + 1, 0, start + each - LANES, value)
            while done < tile or (done in tiles and (done + 1) * LANES <= target + each):
                part = slice(done * LANES, (done + 1) * LANES)
                out_ref[:, part] = (live * (own_ref[:, part] + tiles.pop(done))).astype(out_ref.dtype)
                done += 1


def finish(parts, own, groups, each):
    rows, width = own.shape[0], own.shape[1] - LANES
    return pl.pallas_call(
        functools.partial(finish_kernel, groups, each),
        out_shape=jax.ShapeDtypeStruct((rows, width), jnp.bfloat16),
        in_specs=[pl.BlockSpec(memory_space=pltpu.VMEM)] * 2,
        out_specs=pl.BlockSpec(memory_space=pltpu.VMEM),
        name="finish",
    )(parts, own)


def to_all(x, ranks):
    return lax.all_to_all(jnp.broadcast_to(x[None], (ranks, *x.shape)), "tp", 0, 0)


def shards(residual_rows, norm_gain, gate_weight, up_weight, down_weight, row_count):
    own_rows, width = residual_rows.shape
    ranks, groups = lax.axis_size("tp"), lax.axis_size("dp")
    units, features = down_weight.shape
    each = features // ranks
    resid = residual_rows.astype(jnp.float32)

    split = jnp.pad(down_weight.T.reshape(ranks, each, units), ((0, 0), (0, PADDED - each), (0, 0)))
    mine = lax.all_to_all(split, "tp", 0, 0)
    down = lax.all_gather(mine.reshape(-1, units), "dp", axis=0, tiled=True)

    normed, mine = lax.optimization_barrier((normalize(resid, norm_gain), mine))
    gathered = to_all(normed, ranks).reshape(ranks * own_rows, width)
    gathered, residual_rows, row_count = lax.optimization_barrier((gathered, residual_rows, row_count))
    gate = jnp.dot(gathered, gate_weight, preferred_element_type=jnp.float32)
    up = jnp.dot(gathered, up_weight, preferred_element_type=jnp.float32)
    hidden = (jax.nn.silu(gate) * up).astype(jnp.bfloat16)
    live = lax.broadcasted_iota(jnp.int32, (own_rows, LANES), 0) < row_count[0]
    own = jnp.concatenate([residual_rows.astype(jnp.float32), live.astype(jnp.float32)], axis=1)
    hidden, own = lax.optimization_barrier((hidden.T, own))
    hidden = fetched(to_all(hidden, ranks))

    total = down_projection(hidden, down)
    parts = lax.all_to_all(total.reshape(ranks, own_rows, -1), "tp", 0, 0)
    return finish(parts, own, groups, each)


def solution(mesh):
    return jax.shard_map(
        shards,
        mesh=mesh,
        in_specs=(
            P(("dp", "tp"), None),
            P(),
            P(None, "tp"),
            P(None, "tp"),
            P("tp", "dp"),
            P(("dp", "tp")),
        ),
        out_specs=P(("dp", "tp"), None),
        check_vma=False,
    )
```

```python
import functools

import jax
import jax.numpy as jnp
from jax import lax
from jax.experimental import pallas as pl
from jax.experimental.pallas import tpu as pltpu
from jax.sharding import PartitionSpec as P

LANES = 128
PADDED = 16
CHUNK = 8
VMEM_LIMIT = 46 * 1024 * 1024


def normalize(resid, norm_gain):
    scale = lax.rsqrt(jnp.mean(resid * resid, axis=1, keepdims=True) + 1e-06)
    return (resid * scale * norm_gain[None, :]).astype(jnp.bfloat16)


def fetch_kernel(x_ref, out_ref, sem):
    copy = pltpu.make_async_copy(x_ref, out_ref, sem)
    copy.start()
    copy.wait()


def fetched(x):
    return pl.pallas_call(
        fetch_kernel,
        out_shape=jax.ShapeDtypeStruct(x.shape, x.dtype),
        in_specs=[pl.BlockSpec(memory_space=pl.ANY)],
        out_specs=pl.BlockSpec(memory_space=pltpu.VMEM),
        scratch_shapes=[pltpu.SemaphoreType.DMA],
        compiler_params=pltpu.CompilerParams(vmem_limit_bytes=8 * 1024 * 1024),
        cost_estimate=pl.CostEstimate(flops=0, bytes_accessed=2 * x.size * x.dtype.itemsize, transcendentals=0),
        name="fetched",
    )(x)


def down_kernel(groups, hidden_ref, down_ref, out_ref, held, sems):
    ranks, units = hidden_ref.shape[:2]
    size = CHUNK * ranks * PADDED
    copies = []
    for i in range(groups // CHUNK):
        part = pl.ds(i * size, size)
        copy = pltpu.make_async_copy(down_ref.at[part], held.at[part], sems.at[i])
        copy.start()
        copies.append(copy)
    features = CHUNK * PADDED
    for i, copy in enumerate(copies):
        copy.wait()

        def block(rank):
            starts = [i * size + (group * ranks + rank) * PADDED for group in range(CHUNK)]
            return jnp.concatenate([held[start : start + PADDED, :] for start in starts], axis=0)

        total = None
        for j in range(0, ranks, 2):
            both = jnp.concatenate([block(j), block(j + 1)], axis=1)
            hidden = hidden_ref[j : j + 2].reshape(2 * units, -1)
            terms = jnp.dot(both, hidden, preferred_element_type=jnp.float32)
            total = terms if total is None else total + terms
        out_ref[:, i * features : (i + 1) * features] = total.T


def down_projection(hidden, down):
    ranks, units, rows = hidden.shape
    groups = down.shape[0] // (ranks * PADDED)
    features = groups * PADDED
    return pl.pallas_call(
        functools.partial(down_kernel, groups),
        out_shape=jax.ShapeDtypeStruct((rows, features), jnp.float32),
        in_specs=[pl.BlockSpec(memory_space=pltpu.VMEM), pl.BlockSpec(memory_space=pl.ANY)],
        out_specs=pl.BlockSpec(memory_space=pltpu.VMEM),
        scratch_shapes=[
            pltpu.VMEM(down.shape, jnp.bfloat16),
            pltpu.SemaphoreType.DMA((groups // CHUNK,)),
        ],
        compiler_params=pltpu.CompilerParams(vmem_limit_bytes=VMEM_LIMIT),
        cost_estimate=pl.CostEstimate(
            flops=2 * rows * ranks * units * features,
            bytes_accessed=2 * ranks * units * (features + rows),
            transcendentals=0,
        ),
        name="down_projection",
    )(hidden, down)


def finish_kernel(groups, each, parts_ref, own_ref, out_ref):
    ranks, rows = parts_ref.shape[:2]
    live = own_ref[:, out_ref.shape[1] :]
    lane = lax.broadcasted_iota(jnp.int32, (rows, LANES), 1)
    tiles = {}

    def put(tile, start, stop, value):
        if tile not in tiles:
            tiles[tile] = value
        else:
            tiles[tile] = jnp.where((lane >= start) & (lane < stop), value, tiles[tile])

    done = 0
    for group in range(groups):
        source = group * PADDED
        for rank in range(ranks):
            target = (group * ranks + rank) * each
            tile, start = divmod(target, LANES)
            first = source // LANES * LANES
            value = parts_ref[rank, :, first : first + LANES]
            value = pltpu.roll(value, (start - source % LANES) % LANES, 1)
            put(tile, start, min(start + each, LANES), value)
            if start + each > LANES:
                put(tile + 1, 0, start + each - LANES, value)
            while done < tile or (done in tiles and (done + 1) * LANES <= target + each):
                part = slice(done * LANES, (done + 1) * LANES)
                out_ref[:, part] = (live * (own_ref[:, part] + tiles.pop(done))).astype(out_ref.dtype)
                done += 1


def finish(parts, own, groups, each):
    rows, width = own.shape[0], own.shape[1] - LANES
    return pl.pallas_call(
        functools.partial(finish_kernel, groups, each),
        out_shape=jax.ShapeDtypeStruct((rows, width), jnp.bfloat16),
        in_specs=[pl.BlockSpec(memory_space=pltpu.VMEM)] * 2,
        out_specs=pl.BlockSpec(memory_space=pltpu.VMEM),
        name="finish",
    )(parts, own)


def to_all(x, ranks):
    return lax.all_to_all(jnp.broadcast_to(x[None], (ranks, *x.shape)), "tp", 0, 0)


def shards(residual_rows, norm_gain, gate_weight, up_weight, down_weight, row_count):
    own_rows, width = residual_rows.shape
    ranks, groups = lax.axis_size("tp"), lax.axis_size("dp")
    units, features = down_weight.shape
    each = features // ranks
    resid = residual_rows.astype(jnp.float32)

    split = jnp.pad(down_weight.T.reshape(ranks, each, units), ((0, 0), (0, PADDED - each), (0, 0)))
    mine = lax.all_to_all(split, "tp", 0, 0)
    down = lax.all_gather(mine.reshape(-1, units), "dp", axis=0, tiled=True)

    normed, mine = lax.optimization_barrier((normalize(resid, norm_gain), mine))
    gathered = to_all(normed, ranks).reshape(ranks * own_rows, width)
    gathered, residual_rows, row_count = lax.optimization_barrier((gathered, residual_rows, row_count))
    gate = jnp.dot(gathered, gate_weight, preferred_element_type=jnp.float32)
    up = jnp.dot(gathered, up_weight, preferred_element_type=jnp.float32)
    hidden = (jax.nn.silu(gate) * up).astype(jnp.bfloat16)
    live = lax.broadcasted_iota(jnp.int32, (own_rows, LANES), 0) < row_count[0]
    own = jnp.concatenate([residual_rows.astype(jnp.float32), live.astype(jnp.float32)], axis=1)
    hidden, own = lax.optimization_barrier((hidden.T, own))
    hidden = fetched(to_all(hidden, ranks))

    total = down_projection(hidden, down)
    parts = lax.all_to_all(total.reshape(ranks, own_rows, -1), "tp", 0, 0)
    return finish(parts, own, groups, each)


def solution(mesh):
    return jax.shard_map(
        shards,
        mesh=mesh,
        in_specs=(
            P(("dp", "tp"), None),
            P(),
            P(None, "tp"),
            P(None, "tp"),
            P("tp", "dp"),
            P(("dp", "tp")),
        ),
        out_specs=P(("dp", "tp"), None),
        check_vma=False,
    )
```
